32 devices in a mesh: blk: 2 (over x), stripe: 16 (over z, y, core).
Axes of the slice: x: 2, y: 2, z: 4, core: 2. Of those that a mesh axis runs over, the one named last changes fastest.
Arguments:
- points: bfloat16 [16384, 64], P(('blk', 'stripe')), may hold values from -6 to 6
- coefficients: float32 [16384], P(('blk', 'stripe')), may hold values from -0.09375 to 0.09375
- velocity: float32 [16384], P(('blk', 'stripe')), may hold values from -0.09375 to 0.09375
- targets: float32 [16384], P(('blk', 'stripe')), may hold values from -6 to 6
- batch_rows: int32 [2048], P(('blk', 'stripe')), may hold values from 0 to 511
- counts: int32 [2, 16], P('blk', 'stripe'), may hold values from 1 to 64, 512 in all within a row
Outputs:
- new_coefficients: float32 [16384], P(('blk', 'stripe'))
- new_velocity: float32 [16384], P(('blk', 'stripe'))
The draws below stay inside these ranges and needn't reach their ends.
Inputs may be any that keep to these rules, and one draw needn't show every extreme that they name: In every index of blk, the counts of its 16 devices sum to exactly 512, and some device's count is exactly 64. Only the first count entries of a device's slots are live. `batch_rows`: every entry, live or not, indexes the points of the device that holds it; rows may repeat.
All inputs are finite; a program needn't handle non-finite values.
Results may differ from the reference program's by a relative error of at most 0.0003.
Values may be sent and summed in bfloat16 or wider, within the bound.
No kernel may reach another device: no remote copies, remote signals or barrier semaphores. Data moves between devices by JAX's collectives and lax.ppermute only.
A program may use at most 64 MiB of HBM per device.

```python
import math
import jax
import jax.numpy as jnp
import numpy as np
from jax import lax

D = 64
PTS_DEV = 512
SLOTS = 64
NPTS = 16384
ROWS = 2048
N_BLK = 2
N_STRIPE = 16
DEVICES = 32


def plant(values, own_key, smallest, top_value):
    longest = values.shape.index(max(values.shape))
    spots = []
    for shift in (0, 1):
        where = [jax.random.randint(jax.random.fold_in(own_key, axis), (), 0, length) for axis, length in enumerate(values.shape)]
        where[longest] = (where[longest] + shift) % values.shape[longest]
        spots.append(tuple(where))
    return values.at[spots[0]].set(smallest).at[spots[1]].set(top_value)


def block_scale(own_key, shape, cuts, low, top_value):
    def one(dim, blocks):
        draws = jax.random.uniform(jax.random.fold_in(jax.random.fold_in(own_key, 6), dim), (blocks,), jnp.float32, low / len(cuts), top_value / len(cuts))
        return jnp.repeat(jnp.exp(draws), shape[dim] // blocks).reshape((-1,) + (1,) * (len(shape) - dim - 1))

    gain = one(*cuts[0])
    for cut in cuts[1:]:
        gain = gain * one(*cut)
    return gain


def length_profile(amount, total, reach, lean):
    weights = [(1 << 20) // math.isqrt(rank ** lean) + 1 for rank in range(2, amount + 1)]
    spare, given = total - reach - (amount - 1), [1] * (amount - 1)
    while spare > 0:
        candidates = [i for i in range(amount - 1) if given[i] < reach]
        pool, remaining = sum([weights[i] for i in candidates]), spare
        for i in candidates:
            extra = min(reach - given[i], max(1, remaining * weights[i] // pool), spare)
            given[i] = given[i] + extra
            spare = spare - extra
    return np.array([reach] + given)


def ragged(rng, number_of, total, most, skew):
    if number_of == 2:
        one = jax.random.randint(rng, (), max(1, total - most), min(most, total - 1) + 1)
        return jnp.stack([one, total - one])
    lengths = jnp.asarray(length_profile(number_of, total, most, skew), jnp.int32)
    twos = (number_of - 1) // 2
    donor, sink = lengths[1:1 + 2 * twos:2], lengths[2:2 + 2 * twos:2]
    room = jnp.minimum(donor - 1, most - sink)
    moved = jax.random.randint(jax.random.fold_in(rng, 1), (twos,), 0, 1 << 20) % (room + 1)
    lengths = lengths.at[1:1 + 2 * twos:2].set(donor - moved).at[2:2 + 2 * twos:2].set(sink + moved)
    return lengths[jax.random.permutation(jax.random.fold_in(rng, 2), number_of)]


def gaussian(own_key, dims, scale, reach, shards=(), held_as=jnp.bfloat16):
    values = jax.random.normal(own_key, dims, jnp.float32) * scale
    if len(shards) > 0:
        values = block_scale(own_key, dims, shards, -0.22, 0.18) * values
    return jnp.clip(values, min=-reach, max=reach).astype(held_as)


def setup_inputs(seed: int = 0) -> dict:
    seeds = jax.random.split(jax.random.key(seed), 7)
    return {
        "points": gaussian(seeds[0], (NPTS, D), 1.0, 6.0, ((0, 32),)),
        "coefficients": gaussian(seeds[1], (NPTS,), (NPTS // 4) ** -0.5, 0.09375, ((0, 32),), jnp.float32),
        "velocity": gaussian(seeds[2], (NPTS,), (NPTS // 4) ** -0.5, 0.09375, ((0, 32),), jnp.float32),
        "targets": gaussian(seeds[3], (NPTS,), 1.0, 6.0, ((0, 32),), jnp.float32),
        "batch_rows": plant(jax.random.randint(seeds[4], (ROWS,), 0, PTS_DEV), jax.random.fold_in(seeds[4], 1), 0, PTS_DEV - 1).astype(jnp.int32),
        "counts": jax.vmap(lambda own: ragged(own, N_STRIPE, N_STRIPE * SLOTS // 2, SLOTS, 2))(jax.random.split(seeds[5], N_BLK)).reshape((N_BLK, N_STRIPE)).astype(jnp.int32),
    }


MOMENTUM = 0.9
STEP_SIZE = 1.0
NOISE_VAR = 8.0
KERNEL_RATE = 3.0 ** 0.5 / 6.0

def matern_sums(row_feats, row_sq, col_points, col_coef):
    col_sq = lax.optimization_barrier(jnp.sum(jnp.square(col_points.astype(jnp.float32)), axis=1))
    inner_prod = lax.dot_general(row_feats, col_points, (((1,), (1,)), ((), ())), preferred_element_type=jnp.float32)
    distance = jnp.sqrt(jnp.maximum(row_sq[:, None] + col_sq[None, :] - 2.0 * inner_prod, 0.0))
    scaled = KERNEL_RATE * distance
    kernel_tile = (1.0 + scaled) * jnp.exp(-scaled)
    return lax.optimization_barrier(jnp.sum(kernel_tile * col_coef[None, :], axis=1))

def reference(points, coefficients, velocity, targets, batch_rows, counts):
    preview = coefficients + MOMENTUM * velocity
    device_ids = jnp.arange(DEVICES, dtype=jnp.int32)
    slot_ids = jnp.arange(SLOTS, dtype=jnp.int32)
    point_of = (device_ids[:, None] * PTS_DEV + batch_rows.reshape(DEVICES, SLOTS)).reshape(-1).astype(jnp.int32)
    in_count = (slot_ids[None, :] < counts.reshape(DEVICES, 1)).reshape(-1)
    picked = points[point_of]
    picked_sq = lax.optimization_barrier(jnp.sum(jnp.square(picked.astype(jnp.float32)), axis=1))
    col_block = math.gcd(NPTS, 8192)
    point_blocks = points.reshape(-1, col_block, D)
    coef_blocks = preview.reshape(-1, col_block)
    row_block = math.gcd(ROWS, 2048)

    def block_sums(block_args):
        feat_block, sq_block = block_args

        def advance(partial_sum, column_block):
            return (partial_sum + matern_sums(feat_block, sq_block, column_block[0], column_block[1]), None)
        result, unused = lax.scan(advance, jnp.zeros((feat_block.shape[0],), jnp.float32), (point_blocks, coef_blocks))
        return result
    kernel_sums = lax.map(block_sums, (picked.reshape(-1, row_block, D), picked_sq.reshape(-1, row_block))).reshape(-1)
    residual = jnp.where(in_count, kernel_sums + NOISE_VAR * preview[point_of] - targets[point_of], 0.0)
    update_sum = jnp.zeros((NPTS,), jnp.float32).at[point_of].add(residual)
    new_velocity = MOMENTUM * velocity - STEP_SIZE * update_sum
    new_coefficients = coefficients + new_velocity
    return (new_coefficients, new_velocity)
```

```python
import functools

import jax
import jax.numpy as jnp
from jax import lax
from jax.experimental import pallas as pl
from jax.experimental.pallas import tpu as pltpu
from jax.sharding import PartitionSpec as P

MOMENTUM = 0.9
STEP_SIZE = 1.0
NOISE_VAR = 8.0
KERNEL_RATE = 3.0**0.5 / 6.0
LOG2_E = 1.4426950408889634
AXES = ("blk", "stripe")
SQ_AT, ONE_AT, COEF_AT, EXTRA = 0, 3, 6, 16

F32, BF16 = jnp.float32, jnp.bfloat16


def pieces(value):
    high = value.astype(BF16).astype(F32)
    rest = value - high
    middle = rest.astype(BF16).astype(F32)
    low = (rest - middle).astype(BF16).astype(F32)
    return high, middle, low


def prepare_kernel(points, coef, velocity, targets, batch, count, payload, rows, base, spots):
    size, feats = points.shape
    slots = batch.shape[1]
    preview = coef[...] + MOMENTUM * velocity[...]
    eye = (
        lax.broadcasted_iota(jnp.int32, (feats, feats), 0)
        == lax.broadcasted_iota(jnp.int32, (feats, feats), 1)
    ).astype(BF16)
    turned = lax.dot_general(
        eye, points[...], (((1,), (1,)), ((), ())), preferred_element_type=F32
    )
    col_sq = jnp.sum(turned * turned, axis=0, keepdims=True)
    line = lax.broadcasted_iota(jnp.int32, (EXTRA, size), 0)
    extra = jnp.where((line >= ONE_AT) & (line < ONE_AT + 3), 1.0, 0.0)
    for at, parts in ((SQ_AT, pieces(col_sq)), (COEF_AT, pieces(preview))):
        for k, part in enumerate(parts):
            extra = jnp.where(line == at + k, part, extra)
    payload[...] = jnp.concatenate([turned, extra], axis=0).astype(BF16)
    diagonal = lax.broadcasted_iota(jnp.int32, (slots, slots), 0) == lax.broadcasted_iota(
        jnp.int32, (slots, slots), 1
    )
    column = jnp.sum(jnp.where(diagonal, batch[...].astype(F32), 0.0), axis=1, keepdims=True)
    place = lax.broadcasted_iota(jnp.int32, (slots, size), 1)
    chosen = place == column.astype(jnp.int32)
    picked = jnp.dot(jnp.where(chosen, 1.0, 0.0).astype(BF16), points[...], preferred_element_type=F32)
    row_sq = jnp.sum(picked * picked, axis=1, keepdims=True)
    lane = lax.broadcasted_iota(jnp.int32, (slots, feats), 1)
    tail = jnp.where((lane >= SQ_AT) & (lane < SQ_AT + 3), 1.0, 0.0)
    for k, part in enumerate(pieces(row_sq)):
        tail = jnp.where(lane == ONE_AT + k, part, tail)
    rows[...] = jnp.concatenate([-2.0 * picked, tail], axis=1).astype(BF16)
    live = lax.broadcasted_iota(jnp.int32, (slots, size), 0) < count[0, 0]
    hits = jnp.where(chosen & live, 1.0, 0.0)
    spots[...] = hits.astype(BF16)
    times = jnp.sum(hits, axis=0, keepdims=True)
    base[...] = MOMENTUM * velocity[...] - STEP_SIZE * (
        times * (NOISE_VAR * preview - targets[...])
    )


def sums_kernel(rows, *refs, feats):
    payloads, (keep, send, total) = refs[:-3], refs[-3:]
    depth = feats + EXTRA
    group = 64
    total[...] = jnp.zeros_like(total)
    lane = lax.broadcasted_iota(jnp.int32, (8, depth), 1)
    pick_coef = jnp.where((lane >= feats + COEF_AT) & (lane < feats + COEF_AT + 3), 1.0, 0.0).astype(BF16)
    for payload in payloads:
        block = payload[...]
        weight = jnp.dot(pick_coef, block, preferred_element_type=F32)
        scaled_weight = KERNEL_RATE * weight

        @pl.loop(0, rows.shape[0] // group)
        def _(step):
            start = pl.multiple_of(step * group, group)
            squares = jnp.dot(
                rows[pl.ds(start, group), :][:, :depth], block, preferred_element_type=F32
            )
            for at in range(0, group, 8):
                square = jnp.maximum(squares[at : at + 8, :], 1e-30)
                distance = square * lax.rsqrt(square)
                value = jnp.exp2((-KERNEL_RATE * LOG2_E) * distance) * (
                    weight + scaled_weight * distance
                )
                part = value[:, :128]
                for lanes in range(128, value.shape[1], 128):
                    part = part + value[:, lanes : lanes + 128]
                total[pl.ds(start + at, 8), :] += part

    flat = lax.dot_general(
        jnp.ones((8, 128), F32),
        total[...],
        (((1,), (1,)), ((), ())),
        precision=lax.Precision.HIGHEST,
        preferred_element_type=F32,
    )
    half = keep.shape[1]
    keep[...] = flat[:1, :half]
    send[...] = flat[:1, half:]


def finish_kernel(own, other, base, coef, spots, new_coef, new_velocity):
    slots = spots.shape[0]
    sums = own[...][:, :slots] + other[...]
    line = lax.broadcasted_iota(jnp.int32, (16, slots), 0)
    split = jnp.zeros((16, slots), F32)
    for k, part in enumerate(pieces(sums)):
        split = jnp.where(line == k, part, split)
    update = jnp.dot(split.astype(BF16), spots[...], preferred_element_type=F32)
    velocity = base[...] - STEP_SIZE * jnp.sum(update, axis=0, keepdims=True)
    new_velocity[...] = velocity
    new_coef[...] = coef[...] + velocity


def vmem(count):
    return [pl.BlockSpec(memory_space=pltpu.VMEM)] * count


def per_device(mesh_shape, points, coefficients, velocity, targets, batch_rows, counts):
    n_blk, n_stripe = mesh_shape["blk"], mesh_shape["stripe"]
    size, feats = points.shape
    slots = batch_rows.shape[0]

    def exchange(value, offset):
        d_blk, d_stripe = offset
        pairs = [
            (b * n_stripe + s, (b ^ d_blk) * n_stripe + (s ^ d_stripe))
            for b in range(n_blk)
            for s in range(n_stripe)
        ]
        return lax.ppermute(value, AXES, pairs)

    point_steps = [(1 << k, 1) for k in range(n_blk.bit_length() - 1)] + [(0, 3)]
    row_steps = [(0, 1)] + [(0, (1 << k) + 1) for k in range(2, n_stripe.bit_length() - 1)]

    coef = coefficients.reshape(1, size)
    payload, rows, base, spots = pl.pallas_call(
        prepare_kernel,
        out_shape=[
            jax.ShapeDtypeStruct((feats + EXTRA, size), BF16),
            jax.ShapeDtypeStruct((slots, 2 * feats), BF16),
            jax.ShapeDtypeStruct((1, size), F32),
            jax.ShapeDtypeStruct((slots, size), BF16),
        ],
        in_specs=vmem(5) + [pl.BlockSpec(memory_space=pltpu.SMEM)],
        out_specs=vmem(4),
        name="prepare",
    )(
        points,
        coef,
        velocity.reshape(1, size),
        targets.reshape(1, size),
        batch_rows.reshape(1, slots),
        counts,
    )

    payloads = [payload]
    for step in point_steps:
        payloads = payloads + [exchange(p, step) for p in payloads]
    for step in row_steps:
        rows = jnp.concatenate([rows, exchange(rows, step)], axis=0)

    half = rows.shape[0] // 2
    keep, send = pl.pallas_call(
        functools.partial(sums_kernel, feats=feats),
        out_shape=[jax.ShapeDtypeStruct((1, half), F32)] * 2,
        in_specs=vmem(1 + len(payloads)),
        out_specs=vmem(2),
        scratch_shapes=[pltpu.VMEM((2 * half, 128), F32)],
        compiler_params=pltpu.CompilerParams(vmem_limit_bytes=32 << 20),
        name="kernel_sums",
    )(rows, *payloads)

    for step in row_steps[:0:-1]:
        both = keep + exchange(send, step)
        half = half // 2
        keep, send = both[:, :half], both[:, half:]
    other = exchange(send, row_steps[0])

    new_coef, new_velocity = pl.pallas_call(
        finish_kernel,
        out_shape=[jax.ShapeDtypeStruct((1, size), F32)] * 2,
        in_specs=vmem(5),
        out_specs=vmem(2),
        name="finish",
    )(keep, other, base, coef, spots)
    return new_coef.reshape(size), new_velocity.reshape(size)


def solution(mesh):
    in_specs = (
        P(("blk", "stripe"), None),
        P(("blk", "stripe")),
        P(("blk", "stripe")),
        P(("blk", "stripe")),
        P(("blk", "stripe")),
        P("blk", "stripe"),
    )
    out_specs = (P(("blk", "stripe")), P(("blk", "stripe")))
    return jax.shard_map(
        functools.partial(per_device, dict(mesh.shape)),
        mesh=mesh,
        in_specs=in_specs,
        out_specs=out_specs,
        check_vma=False,
    )
```

```python
import functools

import jax
import jax.numpy as jnp
from jax import lax
from jax.experimental import pallas as pl
from jax.experimental.pallas import tpu as pltpu
from jax.sharding import PartitionSpec as P

MOMENTUM = 0.9
STEP_SIZE = 1.0
NOISE_VAR = 8.0
KERNEL_RATE = 3.0**0.5 / 6.0
LOG2_E = 1.4426950408889634
AXES = ("blk", "stripe")
SQ_AT, ONE_AT, COEF_AT, EXTRA = 0, 3, 6, 16

F32, BF16 = jnp.float32, jnp.bfloat16


def pieces(value):
    high = value.astype(BF16).astype(F32)
    rest = value - high
    middle = rest.astype(BF16).astype(F32)
    low = (rest - middle).astype(BF16).astype(F32)
    return high, middle, low


def prepare_kernel(
    points, coef, velocity, targets, batch, count, payload, rows, base, spots, *scratch
):
    held, sems = scratch[:-1], scratch[-1]
    copies = [
        pltpu.make_async_copy(source, here, sems.at[k])
        for k, (source, here) in enumerate(zip((points, batch, coef, velocity, targets, count), held))
    ]
    for copy in copies:
        copy.start()
    points, batch, coef, velocity, targets, count = held
    feats, size = points.shape
    slots = batch.shape[1]
    copies[1].wait()
    diagonal = lax.broadcasted_iota(jnp.int32, (slots, slots), 0) == lax.broadcasted_iota(
        jnp.int32, (slots, slots), 1
    )
    column = jnp.sum(jnp.where(diagonal, batch[...].astype(F32), 0.0), axis=1, keepdims=True)
    place = lax.broadcasted_iota(jnp.int32, (slots, size), 1)
    chosen = place == column.astype(jnp.int32)
    copies[0].wait()
    feature = points[...]
    picked = lax.dot_general(
        jnp.where(chosen, 1.0, 0.0).astype(BF16),
        feature,
        (((1,), (1,)), ((), ())),
        preferred_element_type=F32,
    )
    row_sq = jnp.sum(picked * picked, axis=1, keepdims=True)
    lane = lax.broadcasted_iota(jnp.int32, (slots, feats), 1)
    tail = jnp.where((lane >= SQ_AT) & (lane < SQ_AT + 3), 1.0, 0.0)
    for k, part in enumerate(pieces(row_sq)):
        tail = jnp.where(lane == ONE_AT + k, part, tail)
    rows[...] = jnp.concatenate([-2.0 * picked, tail], axis=1).astype(BF16)
    payload[:feats, :] = feature
    col_sq = jnp.sum(jnp.square(feature.astype(F32)), axis=0, keepdims=True)
    for copy in copies[2:]:
        copy.wait()
    preview = coef[...] + MOMENTUM * velocity[...]
    line = lax.broadcasted_iota(jnp.int32, (EXTRA, size), 0)
    extra = jnp.where((line >= ONE_AT) & (line < ONE_AT + 3), 1.0, 0.0)
    for at, parts in ((SQ_AT, pieces(col_sq)), (COEF_AT, pieces(preview))):
        for k, part in enumerate(parts):
            extra = jnp.where(line == at + k, part, extra)
    payload[feats:, :] = extra.astype(BF16)
    live = lax.broadcasted_iota(jnp.int32, (slots, 1), 0) < count[...]
    hits = jnp.where(place == jnp.where(live, column, -1.0).astype(jnp.int32), 1.0, 0.0)
    spots[...] = hits.astype(BF16)
    times = jnp.sum(hits, axis=0, keepdims=True)
    base[...] = MOMENTUM * velocity[...] - STEP_SIZE * (
        times * (NOISE_VAR * preview - targets[...])
    )


def sums_kernel(rows, *refs, feats):
    payloads, (keep, send, total) = refs[:-3], refs[-3:]
    depth = feats + EXTRA
    group = min(rows.shape[0], 512)
    total[...] = jnp.zeros_like(total)
    lane = lax.broadcasted_iota(jnp.int32, (8, depth), 1)
    pick_coef = jnp.where((lane >= feats + COEF_AT) & (lane < feats + COEF_AT + 3), 1.0, 0.0).astype(BF16)
    for payload in payloads:
        block = payload[...]
        weight = jnp.dot(pick_coef, block, preferred_element_type=F32)
        scaled_weight = KERNEL_RATE * weight

        @pl.loop(0, rows.shape[0] // group)
        def _(step):
            start = pl.multiple_of(step * group, group)
            squares = jnp.dot(
                rows[pl.ds(start, group), :][:, :depth], block, preferred_element_type=F32
            )
            for at in range(0, group, 8):
                square = jnp.maximum(squares[at : at + 8, :], 1e-30)
                distance = square * lax.rsqrt(square)
                value = jnp.exp2((-KERNEL_RATE * LOG2_E) * distance) * (
                    weight + scaled_weight * distance
                )
                part = value[:, :128]
                for lanes in range(128, value.shape[1], 128):
                    part = part + value[:, lanes : lanes + 128]
                total[pl.ds(start + at, 8), :] += part

    half = keep.shape[1]
    for out, first in ((keep, 0), (send, half)):
        for at in range(0, half, 128):
            turned = total[first + at : first + at + 128, :].T
            out[:, at : at + 128] = jnp.sum(turned, axis=0, keepdims=True)


def finish_kernel(own, other, base, coef, spots, new_coef, new_velocity):
    slots = spots.shape[0]
    sums = own[...][:, :slots] + other[...]
    line = lax.broadcasted_iota(jnp.int32, (16, slots), 0)
    split = jnp.zeros((16, slots), F32)
    for k, part in enumerate(pieces(sums)):
        split = jnp.where(line == k, part, split)
    update = jnp.dot(split.astype(BF16), spots[...], preferred_element_type=F32)
    velocity = base[...] - STEP_SIZE * jnp.sum(update, axis=0, keepdims=True)
    new_velocity[...] = velocity
    new_coef[...] = coef[...] + velocity


def vmem(count):
    return [pl.BlockSpec(memory_space=pltpu.VMEM)] * count


def per_device(mesh_shape, points, coefficients, velocity, targets, batch_rows, counts):
    n_blk, n_stripe = mesh_shape["blk"], mesh_shape["stripe"]
    size, feats = points.shape
    slots = batch_rows.shape[0]

    def exchange(value, offset):
        d_blk, d_stripe = offset
        pairs = [
            (b * n_stripe + s, (b ^ d_blk) * n_stripe + (s ^ d_stripe))
            for b in range(n_blk)
            for s in range(n_stripe)
        ]
        return lax.ppermute(value, AXES, pairs)

    point_steps = [(1 << k, 1) for k in range(n_blk.bit_length() - 1)] + [(0, 3)]
    row_steps = [(0, 1)] + [(0, (1 << k) + 1) for k in range(2, n_stripe.bit_length() - 1)]

    coef = coefficients.reshape(1, size)
    line, spot = (1, size), (1, slots)
    held = [(feats, size), spot, line, line, line, (1, 1)]
    held_types = [BF16, jnp.int32, F32, F32, F32, jnp.int32]
    payload, rows, base, spots = pl.pallas_call(
        prepare_kernel,
        out_shape=[
            jax.ShapeDtypeStruct((feats + EXTRA, size), BF16),
            jax.ShapeDtypeStruct((slots, 2 * feats), BF16),
            jax.ShapeDtypeStruct(line, F32),
            jax.ShapeDtypeStruct((slots, size), BF16),
        ],
        in_specs=[pl.BlockSpec(memory_space=pltpu.HBM)] * 6,
        out_specs=vmem(4),
        scratch_shapes=[pltpu.VMEM(s, t) for s, t in zip(held, held_types)]
        + [pltpu.SemaphoreType.DMA((6,))],
        compiler_params=pltpu.CompilerParams(vmem_limit_bytes=8 << 20),
        name="prepare",
    )(
        points.T,
        coef,
        velocity.reshape(line),
        targets.reshape(line),
        batch_rows.reshape(spot),
        counts,
    )

    payloads = [payload]
    for step in point_steps:
        payloads = payloads + [exchange(p, step) for p in payloads]
    for step in row_steps:
        rows = jnp.concatenate([rows, exchange(rows, step)], axis=0)

    half = rows.shape[0] // 2
    keep, send = pl.pallas_call(
        functools.partial(sums_kernel, feats=feats),
        out_shape=[jax.ShapeDtypeStruct((1, half), F32)] * 2,
        in_specs=vmem(1 + len(payloads)),
        out_specs=vmem(2),
        scratch_shapes=[pltpu.VMEM((2 * half, 128), F32)],
        compiler_params=pltpu.CompilerParams(vmem_limit_bytes=24 << 20),
        name="kernel_sums",
    )(rows, *payloads)

    for step in row_steps[:0:-1]:
        both = keep + exchange(send, step)
        half = half // 2
        keep, send = both[:, :half], both[:, half:]
    other = exchange(send, row_steps[0])

    new_coef, new_velocity = pl.pallas_call(
        finish_kernel,
        out_shape=[jax.ShapeDtypeStruct((1, size), F32)] * 2,
        in_specs=vmem(5),
        out_specs=vmem(2),
        compiler_params=pltpu.CompilerParams(vmem_limit_bytes=8 << 20),
        name="finish",
    )(keep, other, base, coef, spots)
    return new_coef.reshape(size), new_velocity.reshape(size)


def solution(mesh):
    in_specs = (
        P(("blk", "stripe"), None),
        P(("blk", "stripe")),
        P(("blk", "stripe")),
        P(("blk", "stripe")),
        P(("blk", "stripe")),
        P("blk", "stripe"),
    )
    out_specs = (P(("blk", "stripe")), P(("blk", "stripe")))
    return jax.shard_map(
        functools.partial(per_device, dict(mesh.shape)),
        mesh=mesh,
        in_specs=in_specs,
        out_specs=out_specs,
        check_vma=False,
    )
```

```python
import functools

import jax
import jax.numpy as jnp
from jax import lax
from jax.experimental import pallas as pl
from jax.experimental.pallas import tpu as pltpu
from jax.sharding import PartitionSpec as P

MOMENTUM = 0.9
STEP_SIZE = 1.0
NOISE_VAR = 8.0
KERNEL_RATE = 3.0**0.5 / 6.0
LOG2_E = 1.4426950408889634
AXES = ("blk", "stripe")
SQ_AT, ONE_AT, COEF_AT, EXTRA = 0, 3, 6, 16

F32, BF16 = jnp.float32, jnp.bfloat16


def pieces(value):
    high = value.astype(BF16).astype(F32)
    rest = value - high
    middle = rest.astype(BF16).astype(F32)
    low = (rest - middle).astype(BF16).astype(F32)
    return high, middle, low


def payload_kernel(points, coef, velocity, batch, payload, slots):
    feats, size = points.shape
    feature = points[...]
    payload[:feats, :] = feature
    slots[...] = batch[...]
    col_sq = jnp.sum(jnp.square(feature.astype(F32)), axis=0, keepdims=True)
    preview = coef[...] + MOMENTUM * velocity[...]
    line = lax.broadcasted_iota(jnp.int32, (EXTRA, size), 0)
    extra = jnp.where((line >= ONE_AT) & (line < ONE_AT + 3), 1.0, 0.0)
    for at, parts in ((SQ_AT, pieces(col_sq)), (COEF_AT, pieces(preview))):
        for k, part in enumerate(parts):
            extra = jnp.where(line == at + k, part, extra)
    payload[feats:, :] = extra.astype(BF16)


def slot_column(batch):
    slots = batch.shape[1]
    diagonal = lax.broadcasted_iota(jnp.int32, (slots, slots), 0) == lax.broadcasted_iota(
        jnp.int32, (slots, slots), 1
    )
    return jnp.sum(jnp.where(diagonal, batch[...].astype(F32), 0.0), axis=1, keepdims=True)


def rows_kernel(batch, payload, rows):
    feats, size = payload.shape[0] - EXTRA, payload.shape[1]
    slots = batch.shape[1]
    place = lax.broadcasted_iota(jnp.int32, (slots, size), 1)
    chosen = place == slot_column(batch).astype(jnp.int32)
    picked = lax.dot_general(
        jnp.where(chosen, 1.0, 0.0).astype(BF16),
        payload[:feats, :],
        (((1,), (1,)), ((), ())),
        preferred_element_type=F32,
    )
    row_sq = jnp.sum(picked * picked, axis=1, keepdims=True)
    lane = lax.broadcasted_iota(jnp.int32, (slots, feats), 1)
    tail = jnp.where((lane >= SQ_AT) & (lane < SQ_AT + 3), 1.0, 0.0)
    for k, part in enumerate(pieces(row_sq)):
        tail = jnp.where(lane == ONE_AT + k, part, tail)
    rows[...] = jnp.concatenate([-2.0 * picked, tail], axis=1).astype(BF16)


def terms_kernel(batch, coef, velocity, targets, base, spots):
    slots, size = spots.shape
    column = slot_column(batch).astype(jnp.int32)
    place = lax.broadcasted_iota(jnp.int32, (slots, size), 1)
    hits = jnp.where(place == column, 1.0, 0.0)
    spots[...] = hits.astype(BF16)
    times = jnp.sum(hits, axis=0, keepdims=True)
    preview = coef[...] + MOMENTUM * velocity[...]
    base[...] = MOMENTUM * velocity[...] - STEP_SIZE * (
        times * (NOISE_VAR * preview - targets[...])
    )


def sums_kernel(rows, *refs, first):
    if first:
        payloads, (sums, weights, total) = refs[:-3], refs[-3:]
    else:
        weights, payloads, (sums, total) = refs[0], refs[1:-2], refs[-2:]
    amount = rows.shape[0]
    depth = payloads[0].shape[0]
    group = min(amount, 256)
    total[...] = jnp.zeros_like(total)
    if first:
        at = depth - EXTRA + COEF_AT
        lane = lax.broadcasted_iota(jnp.int32, (8, depth), 1)
        pick = jnp.where((lane >= at) & (lane < at + 3), 1.0, 0.0).astype(BF16)
        for k, payload in enumerate(payloads):
            weights[8 * k : 8 * k + 8, :] = jnp.dot(
                pick, payload[...], preferred_element_type=F32
            )
    for k, payload in enumerate(payloads):
        block = payload[...]
        weight = weights[8 * k : 8 * k + 8, :]
        scaled_weight = KERNEL_RATE * weight

        @pl.loop(0, amount // group)
        def _(step):
            start = pl.multiple_of(step * group, group)
            squares = jnp.dot(
                rows[pl.ds(start, group), :][:, :depth], block, preferred_element_type=F32
            )
            for at in range(0, group, 8):
                square = jnp.maximum(squares[at : at + 8, :], 1e-30)
                distance = square * lax.rsqrt(square)
                value = jnp.exp2((-KERNEL_RATE * LOG2_E) * distance) * (
                    weight + scaled_weight * distance
                )
                part = value[:, :128]
                for lanes in range(128, value.shape[1], 128):
                    part = part + value[:, lanes : lanes + 128]
                total[pl.ds(start + at, 8), :] += part

    for at in range(0, amount, 128):
        turned = total[at : at + 128, :].T
        sums[:, at : at + 128] = jnp.sum(turned, axis=0, keepdims=True)


def finish_kernel(own, other, base, coef, spots, new_coef, new_velocity):
    slots = spots.shape[0]
    sums = own[...][:, :slots] + other[...]
    line = lax.broadcasted_iota(jnp.int32, (16, slots), 0)
    split = jnp.zeros((16, slots), F32)
    for k, part in enumerate(pieces(sums)):
        split = jnp.where(line == k, part, split)
    update = jnp.dot(split.astype(BF16), spots[...], preferred_element_type=F32)
    velocity = base[...] - STEP_SIZE * jnp.sum(update, axis=0, keepdims=True)
    new_velocity[...] = velocity
    new_coef[...] = coef[...] + velocity


def call(kernel, name, outs, *operands, limit=8 << 20, scratch=(), cost=None):
    return pl.pallas_call(
        kernel,
        out_shape=[jax.ShapeDtypeStruct(shape, kind) for shape, kind in outs],
        in_specs=[pl.BlockSpec(memory_space=pltpu.VMEM)] * len(operands),
        out_specs=[pl.BlockSpec(memory_space=pltpu.VMEM)] * len(outs),
        scratch_shapes=scratch,
        compiler_params=pltpu.CompilerParams(vmem_limit_bytes=limit),
        cost_estimate=cost,
        name=name,
    )(*operands)


def per_device(mesh_shape, points, coefficients, velocity, targets, batch_rows, counts):
    n_blk, n_stripe = mesh_shape["blk"], mesh_shape["stripe"]
    size, feats = points.shape
    slots = batch_rows.shape[0]

    def exchange(value, offset):
        d_blk, d_stripe = offset
        pairs = [
            (b * n_stripe + s, (b ^ d_blk) * n_stripe + (s ^ d_stripe))
            for b in range(n_blk)
            for s in range(n_stripe)
        ]
        return lax.ppermute(value, AXES, pairs)

    point_steps = [(1 << k, 1) for k in range(n_blk.bit_length() - 1)] + [(0, 3)]
    row_steps = [(0, 1)] + [(0, (1 << k) + 1) for k in range(2, n_stripe.bit_length() - 1)]

    line, spot = (1, size), (1, slots)
    coef, velocity, targets = (x.reshape(line) for x in (coefficients, velocity, targets))
    batch = batch_rows.reshape(spot)
    live = lax.broadcasted_iota(jnp.int32, spot, 1) < counts.reshape(1, 1)
    live_batch = jnp.where(live, batch, -1)
    payload, batch = call(
        payload_kernel,
        "payload",
        [((feats + EXTRA, size), BF16), (spot, jnp.int32)],
        points.T,
        coef,
        velocity,
        batch,
    )
    (rows,) = call(rows_kernel, "rows", [((slots, 2 * feats), BF16)], batch, payload)
    own = payload
    for step in row_steps[:-1]:
        rows = jnp.concatenate([rows, exchange(rows, step)], axis=0)
        if step is row_steps[0]:
            own, rows = lax.optimization_barrier((own, rows))
    more_rows = exchange(rows, row_steps[-1])
    payloads = [payload, exchange(payload, point_steps[0])]
    for step in point_steps[1:]:
        payloads = payloads + [exchange(own if k == 0 else p, step) for k, p in enumerate(payloads)]

    half = rows.shape[0]
    amount = half * size * len(payloads)
    options = dict(
        limit=16 << 20,
        scratch=[pltpu.VMEM((half, 128), F32)],
        cost=pl.CostEstimate(
            flops=2 * feats * amount, bytes_accessed=1 << 16, transcendentals=2 * amount
        ),
    )
    keep, weights = call(
        functools.partial(sums_kernel, first=True),
        "sums_here",
        [((1, half), F32), ((8 * len(payloads), size), F32)],
        rows,
        *payloads,
        **options,
    )
    (send,) = call(
        functools.partial(sums_kernel, first=False),
        "sums_away",
        [((1, half), F32)],
        more_rows,
        weights,
        *payloads,
        **options,
    )
    base, spots = call(
        terms_kernel,
        "terms",
        [(line, F32), ((slots, size), BF16)],
        live_batch,
        coef,
        velocity,
        targets,
    )
    keep, base, spots = lax.optimization_barrier((keep, base, spots))

    for step in row_steps[:0:-1]:
        both = keep + exchange(send, step)
        half = half // 2
        keep, send = both[:, :half], both[:, half:]
    other = exchange(send, row_steps[0])

    new_coef, new_velocity = call(
        finish_kernel, "finish", [(line, F32)] * 2, keep, other, base, coef, spots
    )
    return new_coef.reshape(size), new_velocity.reshape(size)


def solution(mesh):
    in_specs = (
        P(("blk", "stripe"), None),
        P(("blk", "stripe")),
        P(("blk", "stripe")),
        P(("blk", "stripe")),
        P(("blk", "stripe")),
        P("blk", "stripe"),
    )
    out_specs = (P(("blk", "stripe")), P(("blk", "stripe")))
    return jax.shard_map(
        functools.partial(per_device, dict(mesh.shape)),
        mesh=mesh,
        in_specs=in_specs,
        out_specs=out_specs,
        check_vma=False,
    )
```

```python
import functools

import jax
import jax.numpy as jnp
from jax import lax
from jax.experimental import pallas as pl
from jax.experimental.pallas import tpu as pltpu
from jax.sharding import PartitionSpec as P

MOMENTUM = 0.9
STEP_SIZE = 1.0
NOISE_VAR = 8.0
KERNEL_RATE = 3.0**0.5 / 6.0
LOG2_E = 1.4426950408889634
AXES = ("blk", "stripe")
SQ_AT, ONE_AT, COEF_AT, EXTRA = 0, 3, 6, 16

F32, BF16 = jnp.float32, jnp.bfloat16


def pieces(value):
    high = value.astype(BF16).astype(F32)
    rest = value - high
    middle = rest.astype(BF16).astype(F32)
    low = (rest - middle).astype(BF16).astype(F32)
    return high, middle, low


def payload_kernel(points, coef, velocity, batch, payload, slots, *scratch):
    held, sems = scratch[:-1], scratch[-1]
    feats = points.shape[0]
    targets = (payload.at[:feats], *held, slots)
    copies = [
        pltpu.make_async_copy(source, target, sems.at[k])
        for k, (source, target) in enumerate(zip((points, coef, velocity, batch), targets))
    ]
    for copy in copies:
        copy.start()
    for copy in copies:
        copy.wait()
    coef, velocity = held
    size = coef.shape[1]
    feature = payload[:feats, :].astype(F32)
    col_sq = jnp.sum(feature * feature, axis=0, keepdims=True)
    preview = coef[...] + MOMENTUM * velocity[...]
    line = lax.broadcasted_iota(jnp.int32, (EXTRA, size), 0)
    extra = jnp.where((line >= ONE_AT) & (line < ONE_AT + 3), 1.0, 0.0)
    for at, parts in ((SQ_AT, pieces(col_sq)), (COEF_AT, pieces(preview))):
        for k, part in enumerate(parts):
            extra = jnp.where(line == at + k, part, extra)
    payload[feats:, :] = extra.astype(BF16)


def rows_kernel(batch, payload, rows):
    feats, size = payload.shape[0] - EXTRA, payload.shape[1]
    slots = batch.shape[1]
    chosen = lax.broadcasted_iota(jnp.int32, (size, slots), 0) == batch[...]
    rows[...] = jnp.dot(
        payload[:feats, :], jnp.where(chosen, 1.0, 0.0).astype(BF16), preferred_element_type=F32
    ).astype(BF16)


def terms_kernel(batch, coef, velocity, targets, base, spots):
    slots, size = spots.shape
    diagonal = lax.broadcasted_iota(jnp.int32, (slots, slots), 0) == lax.broadcasted_iota(
        jnp.int32, (slots, slots), 1
    )
    column = jnp.sum(jnp.where(diagonal, batch[...].astype(F32), 0.0), axis=1, keepdims=True)
    place = lax.broadcasted_iota(jnp.int32, (slots, size), 1)
    hits = jnp.where(place == column.astype(jnp.int32), 1.0, 0.0)
    spots[...] = hits.astype(BF16)
    times = jnp.sum(hits, axis=0, keepdims=True)
    preview = coef[...] + MOMENTUM * velocity[...]
    base[...] = MOMENTUM * velocity[...] - STEP_SIZE * (
        times * (NOISE_VAR * preview - targets[...])
    )


def sums_kernel(rows, *refs, first):
    if first:
        payloads, (sums, weights, total, left) = refs[:-4], refs[-4:]
    else:
        weights, payloads, (sums, total, left) = refs[0], refs[1:-3], refs[-3:]
    feats, amount = rows.shape
    depth = feats + EXTRA
    group = min(amount, 256)
    for at in range(0, amount, group):
        features = rows[:, at : at + group].astype(F32)
        norms = jnp.sum(features * features, axis=0, keepdims=True)
        line = lax.broadcasted_iota(jnp.int32, (128 - feats, group), 0)
        tail = jnp.where((line >= SQ_AT) & (line < SQ_AT + 3), 1.0, 0.0)
        for k, part in enumerate(pieces(norms)):
            tail = jnp.where(line == ONE_AT + k, part, tail)
        left[at : at + group, :] = jnp.concatenate([-2.0 * features, tail], axis=0).T.astype(BF16)
    total[...] = jnp.zeros_like(total)
    if first:
        at = feats + COEF_AT
        lane = lax.broadcasted_iota(jnp.int32, (8, depth), 1)
        pick = jnp.where((lane >= at) & (lane < at + 3), 1.0, 0.0).astype(BF16)
        for k, payload in enumerate(payloads):
            weights[8 * k : 8 * k + 8, :] = jnp.dot(
                pick, payload[...], preferred_element_type=F32
            )
    for k, payload in enumerate(payloads):
        block = payload[...]
        weight = weights[8 * k : 8 * k + 8, :]
        scaled_weight = KERNEL_RATE * weight

        @pl.loop(0, amount // group)
        def _(step):
            start = pl.multiple_of(step * group, group)
            squares = jnp.dot(
                left[pl.ds(start, group), :][:, :depth], block, preferred_element_type=F32
            )
            for at in range(0, group, 8):
                square = jnp.maximum(squares[at : at + 8, :], 1e-30)
                distance = square * lax.rsqrt(square)
                value = jnp.exp2((-KERNEL_RATE * LOG2_E) * distance) * (
                    weight + scaled_weight * distance
                )
                part = value[:, :128]
                for lanes in range(128, value.shape[1], 128):
                    part = part + value[:, lanes : lanes + 128]
                total[pl.ds(start + at, 8), :] += part

    for at in range(0, amount, 128):
        turned = total[at : at + 128, :].T
        sums[:, at : at + 128] = jnp.sum(turned, axis=0, keepdims=True)


def finish_kernel(own, other, base, coef, spots, new_coef, new_velocity):
    slots = spots.shape[0]
    sums = own[...][:, :slots] + other[...]
    line = lax.broadcasted_iota(jnp.int32, (16, slots), 0)
    split = jnp.zeros((16, slots), F32)
    for k, part in enumerate(pieces(sums)):
        split = jnp.where(line == k, part, split)
    update = jnp.dot(split.astype(BF16), spots[...], preferred_element_type=F32)
    velocity = base[...] - STEP_SIZE * jnp.sum(update, axis=0, keepdims=True)
    new_velocity[...] = velocity
    new_coef[...] = coef[...] + velocity


def call(kernel, name, outs, *operands, limit=8 << 20, scratch=(), cost=None, space=pltpu.VMEM):
    return pl.pallas_call(
        kernel,
        out_shape=[jax.ShapeDtypeStruct(shape, kind) for shape, kind in outs],
        in_specs=[pl.BlockSpec(memory_space=space)] * len(operands),
        out_specs=[pl.BlockSpec(memory_space=pltpu.VMEM)] * len(outs),
        scratch_shapes=scratch,
        compiler_params=pltpu.CompilerParams(vmem_limit_bytes=limit),
        cost_estimate=cost,
        name=name,
    )(*operands)


def per_device(mesh_shape, points, coefficients, velocity, targets, batch_rows, counts):
    n_blk, n_stripe = mesh_shape["blk"], mesh_shape["stripe"]
    size, feats = points.shape
    slots = batch_rows.shape[0]

    def exchange(value, offset):
        d_blk, d_stripe = offset
        pairs = [
            (b * n_stripe + s, (b ^ d_blk) * n_stripe + (s ^ d_stripe))
            for b in range(n_blk)
            for s in range(n_stripe)
        ]
        return lax.ppermute(value, AXES, pairs)

    point_steps = [(1 << k, 1) for k in range(n_blk.bit_length() - 1)] + [(0, 3)]
    row_steps = [(0, 1)] + [(0, (1 << k) + 1) for k in range(2, n_stripe.bit_length() - 1)]

    line, spot = (1, size), (1, slots)
    coef, velocity, targets = (x.reshape(line) for x in (coefficients, velocity, targets))
    batch = batch_rows.reshape(spot)
    live = lax.broadcasted_iota(jnp.int32, spot, 1) < counts.reshape(1, 1)
    live_batch = jnp.where(live, batch, -1)
    payload, batch = call(
        payload_kernel,
        "payload",
        [((feats + EXTRA, size), BF16), (spot, jnp.int32)],
        *(pltpu.with_memory_space_constraint(x, pltpu.HBM) for x in (points.T, coef, velocity, batch)),
        scratch=[pltpu.VMEM(line, F32)] * 2 + [pltpu.SemaphoreType.DMA((4,))],
        space=pltpu.HBM,
    )
    (rows,) = call(rows_kernel, "rows", [((feats, slots), BF16)], batch, payload)
    own = payload
    for step in row_steps[:-1]:
        rows = jnp.concatenate([rows, exchange(rows, step)], axis=1)
        if step is row_steps[0]:
            own, rows = lax.optimization_barrier((own, rows))
    more_rows = exchange(rows, row_steps[-1])
    payloads = [payload, exchange(payload, point_steps[0])]
    for step in point_steps[1:]:
        payloads = payloads + [exchange(own if k == 0 else p, step) for k, p in enumerate(payloads)]

    half = rows.shape[1]
    amount = half * size * len(payloads)
    options = dict(
        limit=16 << 20,
        scratch=[pltpu.VMEM((half, 128), F32), pltpu.VMEM((half, 128), BF16)],
        cost=pl.CostEstimate(
            flops=2 * feats * amount, bytes_accessed=1 << 16, transcendentals=2 * amount
        ),
    )
    keep, weights = call(
        functools.partial(sums_kernel, first=True),
        "sums_here",
        [((1, half), F32), ((8 * len(payloads), size), F32)],
        rows,
        *payloads,
        **options,
    )
    (send,) = call(
        functools.partial(sums_kernel, first=False),
        "sums_away",
        [((1, half), F32)],
        more_rows,
        weights,
        *payloads,
        **options,
    )
    base, spots = call(
        terms_kernel,
        "terms",
        [(line, F32), ((slots, size), BF16)],
        live_batch,
        coef,
        velocity,
        targets,
    )
    keep, base, spots = lax.optimization_barrier((keep, base, spots))

    for step in row_steps[:0:-1]:
        both = keep + exchange(send, step)
        half = half // 2
        keep, send = both[:, :half], both[:, half:]
    other = exchange(send, row_steps[0])

    new_coef, new_velocity = call(
        finish_kernel, "finish", [(line, F32)] * 2, keep, other, base, coef, spots
    )
    return new_coef.reshape(size), new_velocity.reshape(size)


def solution(mesh):
    in_specs = (
        P(("blk", "stripe"), None),
        P(("blk", "stripe")),
        P(("blk", "stripe")),
        P(("blk", "stripe")),
        P(("blk", "stripe")),
        P("blk", "stripe"),
    )
    out_specs = (P(("blk", "stripe")), P(("blk", "stripe")))
    return jax.shard_map(
        functools.partial(per_device, dict(mesh.shape)),
        mesh=mesh,
        in_specs=in_specs,
        out_specs=out_specs,
        check_vma=False,
    )
```

```python
import functools

import jax
import jax.numpy as jnp
from jax import lax
from jax.experimental import pallas as pl
from jax.experimental.pallas import tpu as pltpu
from jax.sharding import PartitionSpec as P

MOMENTUM = 0.9
STEP_SIZE = 1.0
NOISE_VAR = 8.0
KERNEL_RATE = 3.0**0.5 / 6.0
LOG2_E = 1.4426950408889634
AXES = ("blk", "stripe")
SQ_AT, ONE_AT, COEF_AT, EXTRA = 0, 3, 6, 16

F32, BF16 = jnp.float32, jnp.bfloat16


def pieces(value):
    high = value.astype(BF16).astype(F32)
    rest = value - high
    middle = rest.astype(BF16).astype(F32)
    low = (rest - middle).astype(BF16).astype(F32)
    return high, middle, low


def payload_kernel(*refs):
    sources, (payload, slots, preview, slowed, coef, targets), rest = refs[:5], refs[5:11], refs[11:]
    velocity, sems = rest
    feats = sources[0].shape[0]
    copies = [
        pltpu.make_async_copy(source, target, sems.at[k])
        for k, (source, target) in enumerate(
            zip(sources, (payload.at[:feats], slots, coef, velocity, targets))
        )
    ]
    for copy in copies:
        copy.start()
    for copy in copies:
        copy.wait()
    size = coef.shape[1]
    feature = payload[:feats, :].astype(F32)
    col_sq = jnp.sum(feature * feature, axis=0, keepdims=True)
    slowed[...] = MOMENTUM * velocity[...]
    preview[...] = coef[...] + slowed[...]
    line = lax.broadcasted_iota(jnp.int32, (EXTRA, size), 0)
    extra = jnp.where((line >= ONE_AT) & (line < ONE_AT + 3), 1.0, 0.0)
    for at, parts in ((SQ_AT, pieces(col_sq)), (COEF_AT, pieces(preview[...]))):
        for k, part in enumerate(parts):
            extra = jnp.where(line == at + k, part, extra)
    payload[feats:, :] = extra.astype(BF16)


def rows_kernel(batch, payload, rows):
    feats, size = payload.shape[0] - EXTRA, payload.shape[1]
    slots = batch.shape[1]
    chosen = lax.broadcasted_iota(jnp.int32, (size, slots), 0) == batch[...]
    rows[...] = jnp.dot(
        payload[:feats, :], jnp.where(chosen, 1.0, 0.0).astype(BF16), preferred_element_type=F32
    ).astype(BF16)


def terms_kernel(batch, count, preview, slowed, targets, base, spots):
    slots, size = spots.shape
    diagonal = lax.broadcasted_iota(jnp.int32, (slots, slots), 0) == lax.broadcasted_iota(
        jnp.int32, (slots, slots), 1
    )
    live = lax.broadcasted_iota(jnp.int32, (1, slots), 1) < count[:, :1]
    row = jnp.where(live, batch[...], -1).astype(F32)
    column = jnp.sum(jnp.where(diagonal, row, 0.0), axis=1, keepdims=True)
    place = lax.broadcasted_iota(jnp.int32, (slots, size), 1)
    hits = jnp.where(place == column.astype(jnp.int32), 1.0, 0.0)
    spots[...] = hits.astype(BF16)
    times = jnp.sum(hits, axis=0, keepdims=True)
    base[...] = slowed[...] - STEP_SIZE * (times * (NOISE_VAR * preview[...] - targets[...]))


def add_sums(left, payload, total):
    depth = payload.shape[0]
    amount = left.shape[0]
    group = min(amount, 256)
    at = depth - EXTRA + COEF_AT
    lane = lax.broadcasted_iota(jnp.int32, (8, depth), 1)
    pick = jnp.where((lane >= at) & (lane < at + 3), 1.0, 0.0).astype(BF16)
    block = payload[...]
    weight = jnp.dot(pick, block, preferred_element_type=F32)
    scaled_weight = KERNEL_RATE * weight

    def add_group(start):
        squares = jnp.dot(
            left[pl.ds(start, group), :][:, :depth], block, preferred_element_type=F32
        )
        for at in range(0, group, 8):
            square = jnp.maximum(squares[at : at + 8, :], 1e-30)
            distance = square * lax.rsqrt(square)
            value = jnp.exp2((-KERNEL_RATE * LOG2_E) * distance) * (
                weight + scaled_weight * distance
            )
            part = value[:, :128]
            for lanes in range(128, value.shape[1], 128):
                part = part + value[:, lanes : lanes + 128]
            total[pl.ds(start + at, 8), :] += part

    if amount == group:
        add_group(0)
    else:
        pl.loop(0, amount // group)(lambda step: add_group(pl.multiple_of(step * group, group)))


def sums_kernel(rows, *refs):
    payloads, (sums, left, total) = refs[:-3], refs[-3:]
    feats, amount = rows.shape
    group = min(amount, 256)
    for at in range(0, amount, group):
        features = rows[:, at : at + group].astype(F32)
        norms = jnp.sum(features * features, axis=0, keepdims=True)
        line = lax.broadcasted_iota(jnp.int32, (128 - feats, group), 0)
        tail = jnp.where((line >= SQ_AT) & (line < SQ_AT + 3), 1.0, 0.0)
        for k, part in enumerate(pieces(norms)):
            tail = jnp.where(line == ONE_AT + k, part, tail)
        left[at : at + group, :] = jnp.concatenate([-2.0 * features, tail], axis=0).T.astype(BF16)
    total[...] = jnp.zeros_like(total)
    for payload in payloads:
        add_sums(left, payload, total)
    for at in range(0, amount, 128):
        turned = total[at : at + 128, :].T
        sums[:, at : at + 128] = jnp.sum(turned, axis=0, keepdims=True)


def finish_kernel(own, other, base, coef, spots, new_coef, new_velocity):
    slots = spots.shape[0]
    sums = own[...][:, :slots] + other[...]
    line = lax.broadcasted_iota(jnp.int32, (16, slots), 0)
    split = jnp.zeros((16, slots), F32)
    for k, part in enumerate(pieces(sums)):
        split = jnp.where(line == k, part, split)
    update = jnp.dot(split.astype(BF16), spots[...], preferred_element_type=F32)
    velocity = base[...] - STEP_SIZE * jnp.sum(update, axis=0, keepdims=True)
    new_velocity[...] = velocity
    new_coef[...] = coef[...] + velocity


def call(kernel, name, outs, *operands, limit=8 << 20, scratch=(), cost=None, space=pltpu.VMEM):
    return pl.pallas_call(
        kernel,
        out_shape=[jax.ShapeDtypeStruct(shape, kind) for shape, kind in outs],
        in_specs=[pl.BlockSpec(memory_space=space)] * len(operands),
        out_specs=[pl.BlockSpec(memory_space=pltpu.VMEM)] * len(outs),
        scratch_shapes=scratch,
        compiler_params=pltpu.CompilerParams(vmem_limit_bytes=limit),
        cost_estimate=cost,
        name=name,
    )(*operands)


def per_device(mesh_shape, points, coefficients, velocity, targets, batch_rows, counts):
    n_blk, n_stripe = mesh_shape["blk"], mesh_shape["stripe"]
    size, feats = points.shape
    slots = batch_rows.shape[0]

    def exchange(value, offset):
        d_blk, d_stripe = offset
        pairs = [
            (b * n_stripe + s, (b ^ d_blk) * n_stripe + (s ^ d_stripe))
            for b in range(n_blk)
            for s in range(n_stripe)
        ]
        return lax.ppermute(value, AXES, pairs)

    offsets = [(b, s) for s in (0, 2) for b in range(n_blk)]
    point_offsets = [(b, s | 1) for b, s in offsets[1:]]
    row_steps = [(0, (1 << k) + 1) for k in range(n_stripe.bit_length() - 2, 1, -1)]
    other_core = (0, 1)

    line, spot = (1, size), (1, slots)
    batch = batch_rows.reshape(spot)
    vectors = [x.reshape(line) for x in (coefficients, velocity, targets)]
    payload, batch, preview, slowed, coef, targets = call(
        payload_kernel,
        "payload",
        [((feats + EXTRA, size), BF16)] + [(spot, jnp.int32)] + [(line, F32)] * 4,
        *(
            pltpu.with_memory_space_constraint(x, pltpu.HBM)
            for x in (points.T, batch, *vectors)
        ),
        scratch=[
            pltpu.VMEM(line, F32),
            pltpu.SemaphoreType.DMA((5,)),
        ],
        space=pltpu.HBM,
    )
    (rows,) = call(rows_kernel, "rows", [((feats, slots), BF16)], batch, payload)
    beside = exchange(payload, other_core)
    rows, beside = lax.optimization_barrier((rows, beside))
    for step in row_steps[:-1]:
        rows = jnp.concatenate([rows, exchange(rows, step)], axis=1)
    more_rows = exchange(rows, row_steps[-1])
    payloads = [payload] + [exchange(payload, o) for o in point_offsets]
    payloads = payloads + [beside] + [exchange(p, other_core) for p in payloads[1:]]

    half = rows.shape[1]
    amount = half * size * len(payloads)
    cost = pl.CostEstimate(
        flops=2 * feats * amount, bytes_accessed=1 << 16, transcendentals=2 * amount
    )
    (keep,), (send,) = (
        call(
            sums_kernel,
            name,
            [((1, half), F32)],
            some_rows,
            *payloads,
            limit=16 << 20,
            scratch=[pltpu.VMEM((half, 128), BF16), pltpu.VMEM((half, 128), F32)],
            cost=cost,
        )
        for name, some_rows in (("sums_here", rows), ("sums_away", more_rows))
    )
    count = jnp.pad(counts, ((0, 0), (0, slots - counts.shape[1])))
    base, spots = call(
        terms_kernel,
        "terms",
        [(line, F32), ((slots, size), BF16)],
        batch,
        count,
        preview,
        slowed,
        targets,
    )
    keep, base, spots = lax.optimization_barrier((keep, base, spots))

    for step in row_steps[:0:-1]:
        both = keep + exchange(send, step)
        half = half // 2
        keep, send = both[:, :half], both[:, half:]
    other = exchange(send, row_steps[0])

    new_coef, new_velocity = call(
        finish_kernel, "finish", [(line, F32)] * 2, keep, other, base, coef, spots
    )
    return new_coef.reshape(size), new_velocity.reshape(size)


def solution(mesh):
    in_specs = (
        P(("blk", "stripe"), None),
        P(("blk", "stripe")),
        P(("blk", "stripe")),
        P(("blk", "stripe")),
        P(("blk", "stripe")),
        P("blk", "stripe"),
    )
    out_specs = (P(("blk", "stripe")), P(("blk", "stripe")))
    return jax.shard_map(
        functools.partial(per_device, dict(mesh.shape)),
        mesh=mesh,
        in_specs=in_specs,
        out_specs=out_specs,
        check_vma=False,
    )
```

```python
import functools

import jax
import jax.numpy as jnp
from jax import lax
from jax.experimental import pallas as pl
from jax.experimental.pallas import tpu as pltpu
from jax.sharding import PartitionSpec as P

MOMENTUM = 0.9
STEP_SIZE = 1.0
NOISE_VAR = 8.0
KERNEL_RATE = 3.0**0.5 / 6.0
LOG2_E = 1.4426950408889634
AXES = ("blk", "stripe")
SQ_AT, ONE_AT, COEF_AT, EXTRA = 0, 3, 6, 16

F32, BF16 = jnp.float32, jnp.bfloat16


def pieces(value):
    high = value.astype(BF16).astype(F32)
    rest = value - high
    middle = rest.astype(BF16).astype(F32)
    low = (rest - middle).astype(BF16).astype(F32)
    return high, middle, low


def payload_kernel(*refs):
    sources, (payload, slots, preview, slowed, coef, targets), rest = refs[:5], refs[5:11], refs[11:]
    velocity, sems = rest
    feats = sources[0].shape[0]
    copies = [
        pltpu.make_async_copy(source, target, sems.at[k])
        for k, (source, target) in enumerate(
            zip(sources, (payload.at[:feats], slots, coef, velocity, targets))
        )
    ]
    for copy in copies:
        copy.start()
    for copy in copies:
        copy.wait()
    size = coef.shape[1]
    feature = payload[:feats, :].astype(F32)
    col_sq = jnp.sum(feature * feature, axis=0, keepdims=True)
    slowed[...] = MOMENTUM * velocity[...]
    preview[...] = coef[...] + slowed[...]
    line = lax.broadcasted_iota(jnp.int32, (EXTRA, size), 0)
    extra = jnp.where((line >= ONE_AT) & (line < ONE_AT + 3), 1.0, 0.0)
    for at, parts in ((SQ_AT, pieces(col_sq)), (COEF_AT, pieces(preview[...]))):
        for k, part in enumerate(parts):
            extra = jnp.where(line == at + k, part, extra)
    payload[feats:, :] = extra.astype(BF16)


def rows_kernel(batch, payload, rows):
    feats, size = payload.shape[0] - EXTRA, payload.shape[1]
    slots = batch.shape[1]
    chosen = lax.broadcasted_iota(jnp.int32, (size, slots), 0) == batch[...]
    rows[...] = jnp.dot(
        payload[:feats, :], jnp.where(chosen, 1.0, 0.0).astype(BF16), preferred_element_type=F32
    ).astype(BF16)


def terms_kernel(batch, count, preview, slowed, targets, base, spots):
    slots, size = spots.shape
    diagonal = lax.broadcasted_iota(jnp.int32, (slots, slots), 0) == lax.broadcasted_iota(
        jnp.int32, (slots, slots), 1
    )
    live = lax.broadcasted_iota(jnp.int32, (1, slots), 1) < count[:, :1]
    row = jnp.where(live, batch[...], -1).astype(F32)
    column = jnp.sum(jnp.where(diagonal, row, 0.0), axis=1, keepdims=True)
    place = lax.broadcasted_iota(jnp.int32, (slots, size), 1)
    hits = jnp.where(place == column.astype(jnp.int32), 1.0, 0.0)
    spots[...] = hits.astype(BF16)
    times = jnp.sum(hits, axis=0, keepdims=True)
    base[...] = slowed[...] - STEP_SIZE * (times * (NOISE_VAR * preview[...] - targets[...]))


def add_sums(left, payload, total):
    depth = payload.shape[0]
    amount = left.shape[0]
    group = min(amount, 256)
    at = depth - EXTRA + COEF_AT
    lane = lax.broadcasted_iota(jnp.int32, (8, depth), 1)
    pick = jnp.where((lane >= at) & (lane < at + 3), 1.0, 0.0).astype(BF16)
    block = payload[...]
    weight = jnp.dot(pick, block, preferred_element_type=F32)
    scaled_weight = KERNEL_RATE * weight

    def add_group(start):
        squares = jnp.dot(
            left[pl.ds(start, group), :][:, :depth], block, preferred_element_type=F32
        )
        for at in range(0, group, 8):
            square = jnp.maximum(squares[at : at + 8, :], 1e-30)
            distance = square * lax.rsqrt(square)
            value = jnp.exp2((-KERNEL_RATE * LOG2_E) * distance) * (
                weight + scaled_weight * distance
            )
            part = value[:, :128]
            for lanes in range(128, value.shape[1], 128):
                part = part + value[:, lanes : lanes + 128]
            total[pl.ds(start + at, 8), :] += part

    if amount == group:
        add_group(0)
    else:
        pl.loop(0, amount // group)(lambda step: add_group(pl.multiple_of(step * group, group)))


def sums_kernel(rows, *refs):
    payloads, (sums, left, total) = refs[:-3], refs[-3:]
    feats, amount = rows.shape
    group = min(amount, 256)
    for at in range(0, amount, group):
        features = rows[:, at : at + group].astype(F32)
        norms = jnp.sum(features * features, axis=0, keepdims=True)
        line = lax.broadcasted_iota(jnp.int32, (128 - feats, group), 0)
        tail = jnp.where((line >= SQ_AT) & (line < SQ_AT + 3), 1.0, 0.0)
        for k, part in enumerate(pieces(norms)):
            tail = jnp.where(line == ONE_AT + k, part, tail)
        left[at : at + group, :] = jnp.concatenate([-2.0 * features, tail], axis=0).T.astype(BF16)
    total[...] = jnp.zeros_like(total)
    for payload in payloads:
        add_sums(left, payload, total)
    for at in range(0, amount, 128):
        turned = total[at : at + 128, :].T
        sums[:, at : at + 128] = jnp.sum(turned, axis=0, keepdims=True)


def finish_kernel(own, other, base, coef, spots, new_coef, new_velocity):
    slots = spots.shape[0]
    sums = own[...][:, :slots] + other[...]
    line = lax.broadcasted_iota(jnp.int32, (16, slots), 0)
    split = jnp.zeros((16, slots), F32)
    for k, part in enumerate(pieces(sums)):
        split = jnp.where(line == k, part, split)
    update = jnp.dot(split.astype(BF16), spots[...], preferred_element_type=F32)
    velocity = base[...] - STEP_SIZE * jnp.sum(update, axis=0, keepdims=True)
    new_velocity[...] = velocity
    new_coef[...] = coef[...] + velocity


def call(kernel, name, outs, *operands, limit=8 << 20, scratch=(), cost=None, space=pltpu.VMEM):
    return pl.pallas_call(
        kernel,
        out_shape=[jax.ShapeDtypeStruct(shape, kind) for shape, kind in outs],
        in_specs=[pl.BlockSpec(memory_space=space)] * len(operands),
        out_specs=[pl.BlockSpec(memory_space=pltpu.VMEM)] * len(outs),
        scratch_shapes=scratch,
        compiler_params=pltpu.CompilerParams(vmem_limit_bytes=limit),
        cost_estimate=cost,
        name=name,
    )(*operands)


def per_device(mesh_shape, points, coefficients, velocity, targets, batch_rows, counts):
    n_blk, n_stripe = mesh_shape["blk"], mesh_shape["stripe"]
    size, feats = points.shape
    slots = batch_rows.shape[0]

    def exchange(value, offset):
        d_blk, d_stripe = offset
        pairs = [
            (b * n_stripe + s, (b ^ d_blk) * n_stripe + (s ^ d_stripe))
            for b in range(n_blk)
            for s in range(n_stripe)
        ]
        return lax.ppermute(value, AXES, pairs)

    offsets = [(b, s) for s in (0, 2) for b in range(n_blk)]
    point_offsets = [(b, s | 1) for b, s in offsets[:0:-1]]
    row_steps = [(0, (1 << k) + 1) for k in range(n_stripe.bit_length() - 2, 1, -1)]
    other_core = (0, 1)

    line, spot = (1, size), (1, slots)
    batch = batch_rows.reshape(spot)
    vectors = [x.reshape(line) for x in (coefficients, velocity, targets)]
    payload, batch, preview, slowed, coef, targets = call(
        payload_kernel,
        "payload",
        [((feats + EXTRA, size), BF16)] + [(spot, jnp.int32)] + [(line, F32)] * 4,
        *(
            pltpu.with_memory_space_constraint(x, pltpu.HBM)
            for x in (points.T, batch, *vectors)
        ),
        scratch=[
            pltpu.VMEM(line, F32),
            pltpu.SemaphoreType.DMA((5,)),
        ],
        space=pltpu.HBM,
    )
    (rows,) = call(rows_kernel, "rows", [((feats, slots), BF16)], batch, payload)
    beside = exchange(payload, other_core)
    for step in row_steps[:-1]:
        rows = jnp.concatenate([rows, exchange(rows, step)], axis=1)
    more_rows = exchange(rows, row_steps[-1])
    payloads = [payload] + [exchange(payload, o) for o in point_offsets]
    payloads = payloads + [beside] + [exchange(p, other_core) for p in payloads[1:]]

    half = rows.shape[1]
    amount = half * size * len(payloads)
    cost = pl.CostEstimate(
        flops=2 * feats * amount, bytes_accessed=1 << 16, transcendentals=2 * amount
    )
    (keep,), (send,) = (
        call(
            sums_kernel,
            name,
            [((1, half), F32)],
            some_rows,
            *payloads,
            limit=16 << 20,
            scratch=[pltpu.VMEM((half, 128), BF16), pltpu.VMEM((half, 128), F32)],
            cost=cost,
        )
        for name, some_rows in (("sums_here", rows), ("sums_away", more_rows))
    )
    count = jnp.pad(counts, ((0, 0), (0, slots - counts.shape[1])))
    base, spots = call(
        terms_kernel,
        "terms",
        [(line, F32), ((slots, size), BF16)],
        batch,
        count,
        preview,
        slowed,
        targets,
    )
    keep, base, spots = lax.optimization_barrier((keep, base, spots))

    for step in row_steps[:0:-1]:
        both = keep + exchange(send, step)
        half = half // 2
        keep, send = both[:, :half], both[:, half:]
    other = exchange(send, row_steps[0])

    new_coef, new_velocity = call(
        finish_kernel, "finish", [(line, F32)] * 2, keep, other, base, coef, spots
    )
    return new_coef.reshape(size), new_velocity.reshape(size)


def solution(mesh):
    in_specs = (
        P(("blk", "stripe"), None),
        P(("blk", "stripe")),
        P(("blk", "stripe")),
        P(("blk", "stripe")),
        P(("blk", "stripe")),
        P("blk", "stripe"),
    )
    out_specs = (P(("blk", "stripe")), P(("blk", "stripe")))
    return jax.shard_map(
        functools.partial(per_device, dict(mesh.shape)),
        mesh=mesh,
        in_specs=in_specs,
        out_specs=out_specs,
        check_vma=False,
    )
```

```python
import functools

import jax
import jax.numpy as jnp
from jax import lax
from jax.experimental import pallas as pl
from jax.experimental.pallas import tpu as pltpu
from jax.sharding import PartitionSpec as P

MOMENTUM = 0.9
STEP_SIZE = 1.0
NOISE_VAR = 8.0
KERNEL_RATE = 3.0**0.5 / 6.0
LOG2_E = 1.4426950408889634
AXES = ("blk", "stripe")
SQ_AT, ONE_AT, COEF_AT, EXTRA = 0, 3, 6, 16

F32, BF16 = jnp.float32, jnp.bfloat16


def pieces(value):
    high = value.astype(BF16).astype(F32)
    rest = value - high
    middle = rest.astype(BF16).astype(F32)
    low = (rest - middle).astype(BF16).astype(F32)
    return high, middle, low


def payload_kernel(*refs):
    sources, (payload, slots, preview, slowed, coef, targets), rest = refs[:5], refs[5:11], refs[11:]
    velocity, sems = rest
    feats = sources[0].shape[0]
    copies = [
        pltpu.make_async_copy(source, target, sems.at[k])
        for k, (source, target) in enumerate(
            zip(sources, (payload.at[:feats], slots, coef, velocity, targets))
        )
    ]
    for copy in copies:
        copy.start()
    for copy in copies:
        copy.wait()
    size = coef.shape[1]
    feature = payload[:feats, :].astype(F32)
    col_sq = jnp.sum(feature * feature, axis=0, keepdims=True)
    slowed[...] = MOMENTUM * velocity[...]
    preview[...] = coef[...] + slowed[...]
    line = lax.broadcasted_iota(jnp.int32, (EXTRA, size), 0)
    extra = jnp.where((line >= ONE_AT) & (line < ONE_AT + 3), 1.0, 0.0)
    for at, parts in ((SQ_AT, pieces(col_sq)), (COEF_AT, pieces(preview[...]))):
        for k, part in enumerate(parts):
            extra = jnp.where(line == at + k, part, extra)
    payload[feats:, :] = extra.astype(BF16)


def rows_kernel(batch, payload, rows):
    feats, size = payload.shape[0] - EXTRA, payload.shape[1]
    slots = batch.shape[1]
    chosen = lax.broadcasted_iota(jnp.int32, (size, slots), 0) == batch[...]
    rows[...] = jnp.dot(
        payload[:feats, :], jnp.where(chosen, 1.0, 0.0).astype(BF16), preferred_element_type=F32
    ).astype(BF16)


def terms_kernel(batch, count, preview, slowed, targets, after, base, spots):
    slots, size = spots.shape
    diagonal = lax.broadcasted_iota(jnp.int32, (slots, slots), 0) == lax.broadcasted_iota(
        jnp.int32, (slots, slots), 1
    )
    live = lax.broadcasted_iota(jnp.int32, (1, slots), 1) < count[:, :1]
    row = jnp.where(live, batch[...], -1).astype(F32)
    column = jnp.sum(jnp.where(diagonal, row, 0.0), axis=1, keepdims=True)
    place = lax.broadcasted_iota(jnp.int32, (slots, size), 1)
    hits = jnp.where(place == column.astype(jnp.int32), 1.0, 0.0)
    spots[...] = hits.astype(BF16)
    times = jnp.sum(hits, axis=0, keepdims=True)
    base[...] = slowed[...] - STEP_SIZE * (times * (NOISE_VAR * preview[...] - targets[...]))


def add_sums(left, payload, total):
    depth = payload.shape[0]
    amount = left.shape[0]
    group = min(amount, 256)
    at = depth - EXTRA + COEF_AT
    lane = lax.broadcasted_iota(jnp.int32, (8, depth), 1)
    pick = jnp.where((lane >= at) & (lane < at + 3), 1.0, 0.0).astype(BF16)
    block = payload[...]
    weight = jnp.dot(pick, block, preferred_element_type=F32)
    scaled_weight = KERNEL_RATE * weight

    def add_group(start):
        squares = jnp.dot(
            left[pl.ds(start, group), :][:, :depth], block, preferred_element_type=F32
        )
        for at in range(0, group, 8):
            square = jnp.maximum(squares[at : at + 8, :], 1e-30)
            distance = square * lax.rsqrt(square)
            value = jnp.exp2((-KERNEL_RATE * LOG2_E) * distance) * (
                weight + scaled_weight * distance
            )
            part = value[:, :128]
            for lanes in range(128, value.shape[1], 128):
                part = part + value[:, lanes : lanes + 128]
            total[pl.ds(start + at, 8), :] += part

    if amount == group:
        add_group(0)
    else:
        pl.loop(0, amount // group)(lambda step: add_group(pl.multiple_of(step * group, group)))


def turn_rows(rows, left):
    feats, amount = rows.shape
    group = min(amount, 256)
    for at in range(0, amount, group):
        features = rows[:, at : at + group].astype(F32)
        norms = jnp.sum(features * features, axis=0, keepdims=True)
        line = lax.broadcasted_iota(jnp.int32, (128 - feats, group), 0)
        tail = jnp.where((line >= SQ_AT) & (line < SQ_AT + 3), 1.0, 0.0)
        for k, part in enumerate(pieces(norms)):
            tail = jnp.where(line == ONE_AT + k, part, tail)
        left[at : at + group, :] = jnp.concatenate([-2.0 * features, tail], axis=0).T.astype(BF16)


def row_sums(left, payloads, total):
    total[...] = jnp.zeros_like(total)
    for payload in payloads:
        add_sums(left, payload, total)
    amount = total.shape[0]
    width = min(amount, 128)
    parts = [
        jnp.sum(total[at : at + width, :].T, axis=0, keepdims=True)
        for at in range(0, amount, width)
    ]
    return parts[0] if len(parts) == 1 else jnp.concatenate(parts, axis=1)


def here_kernel(rows, *refs):
    payloads, (sums, left, total) = refs[:-3], refs[-3:]
    turn_rows(rows, left)
    sums[...] = row_sums(left, payloads, total)


def send_kernel(rows, here, *refs):
    payloads, (sums, left, total) = refs[:-3], refs[-3:]
    half = total.shape[0]
    turn_rows(rows, left)
    mine = row_sums(left.at[half : 2 * half], payloads, total)
    sums[...] = jnp.concatenate([here[:, half:], mine], axis=1)


def keep_kernel(rows, *refs):
    payloads, (sums, left, total) = refs[:-3], refs[-3:]
    turn_rows(rows, left)
    sums[...] = row_sums(left.at[: total.shape[0]], payloads, total)


def finish_kernel(own, other, base, coef, spots, new_coef, new_velocity):
    slots = spots.shape[0]
    sums = own[...][:, :slots] + other[...]
    line = lax.broadcasted_iota(jnp.int32, (16, slots), 0)
    split = jnp.zeros((16, slots), F32)
    for k, part in enumerate(pieces(sums)):
        split = jnp.where(line == k, part, split)
    update = jnp.dot(split.astype(BF16), spots[...], preferred_element_type=F32)
    velocity = base[...] - STEP_SIZE * jnp.sum(update, axis=0, keepdims=True)
    new_velocity[...] = velocity
    new_coef[...] = coef[...] + velocity


def call(kernel, name, outs, *operands, limit=8 << 20, scratch=(), cost=None, space=pltpu.VMEM):
    return pl.pallas_call(
        kernel,
        out_shape=[jax.ShapeDtypeStruct(shape, kind) for shape, kind in outs],
        in_specs=[pl.BlockSpec(memory_space=space)] * len(operands),
        out_specs=[pl.BlockSpec(memory_space=pltpu.VMEM)] * len(outs),
        scratch_shapes=scratch,
        compiler_params=pltpu.CompilerParams(vmem_limit_bytes=limit),
        cost_estimate=cost,
        name=name,
    )(*operands)


def per_device(mesh_shape, points, coefficients, velocity, targets, batch_rows, counts):
    n_blk, n_stripe = mesh_shape["blk"], mesh_shape["stripe"]
    size, feats = points.shape
    slots = batch_rows.shape[0]

    def exchange(value, offset):
        d_blk, d_stripe = offset
        pairs = [
            (b * n_stripe + s, (b ^ d_blk) * n_stripe + (s ^ d_stripe))
            for b in range(n_blk)
            for s in range(n_stripe)
        ]
        return lax.ppermute(value, AXES, pairs)

    offsets = [(b, s) for s in (0, 2) for b in range(n_blk)]
    point_offsets = [(b, s | 1) for b, s in offsets[1:]]
    row_steps = [(0, (1 << k) + 1) for k in range(n_stripe.bit_length() - 2, 1, -1)]
    other_core = (0, 1)

    line, spot = (1, size), (1, slots)
    batch = batch_rows.reshape(spot)
    vectors = [x.reshape(line) for x in (coefficients, velocity, targets)]
    payload, batch, preview, slowed, coef, targets = call(
        payload_kernel,
        "payload",
        [((feats + EXTRA, size), BF16)] + [(spot, jnp.int32)] + [(line, F32)] * 4,
        *(
            pltpu.with_memory_space_constraint(x, pltpu.HBM)
            for x in (points.T, batch, *vectors)
        ),
        scratch=[
            pltpu.VMEM(line, F32),
            pltpu.SemaphoreType.DMA((5,)),
        ],
        space=pltpu.HBM,
    )
    (rows,) = call(rows_kernel, "rows", [((feats, slots), BF16)], batch, payload)
    beside = exchange(payload, other_core)
    halves = [rows, exchange(rows, row_steps[0])]
    rows = jnp.concatenate(halves, axis=1)
    for step in row_steps[1:-1]:
        other = exchange(rows, step)
        split = other.shape[1] // 2
        halves = [
            jnp.concatenate([halves[0], other[:, :split]], axis=1),
            jnp.concatenate([halves[1], other[:, split:]], axis=1),
        ]
        rows = jnp.concatenate(halves, axis=1)
    more_rows = exchange(rows, row_steps[-1])
    payloads = [payload] + [exchange(payload, o) for o in point_offsets]
    payloads = payloads + [beside] + [exchange(p, other_core) for p in payloads[1:]]

    amount = rows.shape[1]
    half = amount // 2

    def sums(kernel, name, outs, kept, *operands):
        work = kept * size * len(payloads)
        return call(
            kernel,
            name,
            [((1, outs), F32)],
            *operands,
            *payloads,
            limit=16 << 20,
            scratch=[pltpu.VMEM((amount, 128), BF16), pltpu.VMEM((kept, 128), F32)],
            cost=pl.CostEstimate(
                flops=2 * feats * work, bytes_accessed=1 << 16, transcendentals=2 * work
            ),
        )[0]

    here = sums(here_kernel, "sums_here", amount, amount, rows)
    send = sums(send_kernel, "sums_send", amount, half, more_rows, here)
    keep = sums(keep_kernel, "sums_keep", half, half, more_rows)
    count = jnp.pad(counts, ((0, 0), (0, slots - counts.shape[1])))
    base, spots = call(
        terms_kernel,
        "terms",
        [(line, F32), ((slots, size), BF16)],
        batch,
        count,
        preview,
        slowed,
        targets,
        keep,
    )
    keep, base, spots = lax.optimization_barrier((keep, base, spots))

    back = exchange(send, row_steps[0])
    mine, send = here[:, :half] + back[:, :half], keep + back[:, half:]
    steps = [row_steps[-1]] + row_steps[1:-1][::-1]
    for step in steps[:-1]:
        both = mine + exchange(send, step)
        half = half // 2
        mine, send = both[:, :half], both[:, half:]
    other = exchange(send, steps[-1])

    new_coef, new_velocity = call(
        finish_kernel, "finish", [(line, F32)] * 2, mine, other, base, coef, spots
    )
    return new_coef.reshape(size), new_velocity.reshape(size)


def solution(mesh):
    in_specs = (
        P(("blk", "stripe"), None),
        P(("blk", "stripe")),
        P(("blk", "stripe")),
        P(("blk", "stripe")),
        P(("blk", "stripe")),
        P("blk", "stripe"),
    )
    out_specs = (P(("blk", "stripe")), P(("blk", "stripe")))
    return jax.shard_map(
        functools.partial(per_device, dict(mesh.shape)),
        mesh=mesh,
        in_specs=in_specs,
        out_specs=out_specs,
        check_vma=False,
    )
```

```python
import functools

import jax
import jax.numpy as jnp
from jax import lax
from jax.experimental import pallas as pl
from jax.experimental.pallas import tpu as pltpu
from jax.sharding import PartitionSpec as P

MOMENTUM = 0.9
STEP_SIZE = 1.0
NOISE_VAR = 8.0
KERNEL_RATE = 3.0**0.5 / 6.0
LOG2_E = 1.4426950408889634
AXES = ("blk", "stripe")
SQ_AT, ONE_AT, COEF_AT, EXTRA = 0, 3, 6, 16

F32, BF16 = jnp.float32, jnp.bfloat16


def pieces(value):
    high = value.astype(BF16).astype(F32)
    rest = value - high
    middle = rest.astype(BF16).astype(F32)
    low = (rest - middle).astype(BF16).astype(F32)
    return high, middle, low


def payload_kernel(*refs):
    sources, (payload, slots, preview, slowed, coef, targets), rest = refs[:5], refs[5:11], refs[11:]
    velocity, sems = rest
    feats = sources[0].shape[0]
    copies = [
        pltpu.make_async_copy(source, target, sems.at[k])
        for k, (source, target) in enumerate(
            zip(sources, (payload.at[:feats], slots, coef, velocity, targets))
        )
    ]
    for copy in copies:
        copy.start()
    for copy in copies:
        copy.wait()
    size = coef.shape[1]
    feature = payload[:feats, :].astype(F32)
    col_sq = jnp.sum(feature * feature, axis=0, keepdims=True)
    slowed[...] = MOMENTUM * velocity[...]
    preview[...] = coef[...] + slowed[...]
    line = lax.broadcasted_iota(jnp.int32, (EXTRA, size), 0)
    extra = jnp.where((line >= ONE_AT) & (line < ONE_AT + 3), 1.0, 0.0)
    for at, parts in ((SQ_AT, pieces(col_sq)), (COEF_AT, pieces(preview[...]))):
        for k, part in enumerate(parts):
            extra = jnp.where(line == at + k, part, extra)
    payload[feats:, :] = extra.astype(BF16)


def rows_kernel(batch, payload, rows):
    feats, size = payload.shape[0] - EXTRA, payload.shape[1]
    slots = batch.shape[1]
    chosen = lax.broadcasted_iota(jnp.int32, (size, slots), 0) == batch[...]
    rows[...] = jnp.dot(
        payload[:feats, :], jnp.where(chosen, 1.0, 0.0).astype(BF16), preferred_element_type=F32
    ).astype(BF16)


def terms_kernel(batch, count, preview, slowed, targets, after, base, spots):
    slots, size = spots.shape
    diagonal = lax.broadcasted_iota(jnp.int32, (slots, slots), 0) == lax.broadcasted_iota(
        jnp.int32, (slots, slots), 1
    )
    live = lax.broadcasted_iota(jnp.int32, (1, slots), 1) < count[:, :1]
    row = jnp.where(live, batch[...], -1).astype(F32)
    column = jnp.sum(jnp.where(diagonal, row, 0.0), axis=1, keepdims=True)
    place = lax.broadcasted_iota(jnp.int32, (slots, size), 1)
    hits = jnp.where(place == column.astype(jnp.int32), 1.0, 0.0)
    spots[...] = hits.astype(BF16)
    times = jnp.sum(hits, axis=0, keepdims=True)
    base[...] = slowed[...] - STEP_SIZE * (times * (NOISE_VAR * preview[...] - targets[...]))


def add_sums(left, payload, weight, total):
    depth = payload.shape[0]
    amount = left.shape[0]
    group = min(amount, 256)
    block = payload[...]
    scaled_weight = KERNEL_RATE * weight

    def add_group(start):
        squares = jnp.dot(
            left[pl.ds(start, group), :][:, :depth], block, preferred_element_type=F32
        )
        for at in range(0, group, 8):
            square = jnp.maximum(squares[at : at + 8, :], 1e-30)
            distance = square * lax.rsqrt(square)
            value = jnp.exp2((-KERNEL_RATE * LOG2_E) * distance) * (
                weight + scaled_weight * distance
            )
            part = value[:, :128]
            for lanes in range(128, value.shape[1], 128):
                part = part + value[:, lanes : lanes + 128]
            total[pl.ds(start + at, 8), :] += part

    if amount == group:
        add_group(0)
    else:
        pl.loop(0, amount // group)(lambda step: add_group(pl.multiple_of(step * group, group)))


def turn_rows(rows, left):
    feats, amount = rows.shape
    group = min(amount, 256)
    for at in range(0, amount, group):
        features = rows[:, at : at + group].astype(F32)
        norms = jnp.sum(features * features, axis=0, keepdims=True)
        line = lax.broadcasted_iota(jnp.int32, (128 - feats, group), 0)
        tail = jnp.where((line >= SQ_AT) & (line < SQ_AT + 3), 1.0, 0.0)
        for k, part in enumerate(pieces(norms)):
            tail = jnp.where(line == ONE_AT + k, part, tail)
        left[at : at + group, :] = jnp.concatenate([-2.0 * features, tail], axis=0).T.astype(BF16)


def row_sums(left, payloads, weights, total):
    total[...] = jnp.zeros_like(total)
    for k, payload in enumerate(payloads):
        add_sums(left, payload, weights[8 * k : 8 * k + 8, :], total)
    amount = total.shape[0]
    width = min(amount, 128)
    parts = [
        jnp.sum(total[at : at + width, :].T, axis=0, keepdims=True)
        for at in range(0, amount, width)
    ]
    return parts[0] if len(parts) == 1 else jnp.concatenate(parts, axis=1)


def here_kernel(rows, *refs):
    payloads, (sums, weights, left, total) = refs[:-4], refs[-4:]
    turn_rows(rows, left)
    depth = payloads[0].shape[0]
    at = depth - EXTRA + COEF_AT
    lane = lax.broadcasted_iota(jnp.int32, (8, depth), 1)
    pick = jnp.where((lane >= at) & (lane < at + 3), 1.0, 0.0).astype(BF16)
    for k, payload in enumerate(payloads):
        weights[8 * k : 8 * k + 8, :] = jnp.dot(pick, payload[...], preferred_element_type=F32)
    sums[...] = row_sums(left, payloads, weights, total)


def send_kernel(rows, here, weights, *refs):
    payloads, (sums, left, total) = refs[:-3], refs[-3:]
    half = total.shape[0]
    turn_rows(rows, left)
    mine = row_sums(left.at[half : 2 * half], payloads, weights, total)
    sums[...] = jnp.concatenate([here[:, half:], mine], axis=1)


def keep_kernel(rows, weights, *refs):
    payloads, (sums, left, total) = refs[:-3], refs[-3:]
    turn_rows(rows, left)
    sums[...] = row_sums(left.at[: total.shape[0]], payloads, weights, total)


def finish_kernel(own, other, base, coef, spots, new_coef, new_velocity):
    slots = spots.shape[0]
    sums = own[...][:, :slots] + other[...]
    line = lax.broadcasted_iota(jnp.int32, (16, slots), 0)
    split = jnp.zeros((16, slots), F32)
    for k, part in enumerate(pieces(sums)):
        split = jnp.where(line == k, part, split)
    update = jnp.dot(split.astype(BF16), spots[...], preferred_element_type=F32)
    velocity = base[...] - STEP_SIZE * jnp.sum(update, axis=0, keepdims=True)
    new_velocity[...] = velocity
    new_coef[...] = coef[...] + velocity


def call(kernel, name, outs, *operands, limit=8 << 20, scratch=(), cost=None, space=pltpu.VMEM):
    return pl.pallas_call(
        kernel,
        out_shape=[jax.ShapeDtypeStruct(shape, kind) for shape, kind in outs],
        in_specs=[pl.BlockSpec(memory_space=space)] * len(operands),
        out_specs=[pl.BlockSpec(memory_space=pltpu.VMEM)] * len(outs),
        scratch_shapes=scratch,
        compiler_params=pltpu.CompilerParams(vmem_limit_bytes=limit),
        cost_estimate=cost,
        name=name,
    )(*operands)


def per_device(mesh_shape, points, coefficients, velocity, targets, batch_rows, counts):
    n_blk, n_stripe = mesh_shape["blk"], mesh_shape["stripe"]
    size, feats = points.shape
    slots = batch_rows.shape[0]

    def exchange(value, offset):
        d_blk, d_stripe = offset
        pairs = [
            (b * n_stripe + s, (b ^ d_blk) * n_stripe + (s ^ d_stripe))
            for b in range(n_blk)
            for s in range(n_stripe)
        ]
        return lax.ppermute(value, AXES, pairs)

    offsets = [(b, s) for s in (0, 2) for b in range(n_blk)]
    point_offsets = [(b, s | 1) for b, s in offsets[1:]]
    row_steps = [(0, (1 << k) + 1) for k in range(n_stripe.bit_length() - 2, 1, -1)]
    other_core = (0, 1)

    line, spot = (1, size), (1, slots)
    batch = batch_rows.reshape(spot)
    vectors = [x.reshape(line) for x in (coefficients, velocity, targets)]
    payload, batch, preview, slowed, coef, targets = call(
        payload_kernel,
        "payload",
        [((feats + EXTRA, size), BF16)] + [(spot, jnp.int32)] + [(line, F32)] * 4,
        *(
            pltpu.with_memory_space_constraint(x, pltpu.HBM)
            for x in (points.T, batch, *vectors)
        ),
        scratch=[
            pltpu.VMEM(line, F32),
            pltpu.SemaphoreType.DMA((5,)),
        ],
        space=pltpu.HBM,
    )
    (rows,) = call(rows_kernel, "rows", [((feats, slots), BF16)], batch, payload)
    beside = exchange(payload, other_core)
    halves = [rows, exchange(rows, row_steps[0])]
    rows = jnp.concatenate(halves, axis=1)
    for step in row_steps[1:-1]:
        other = exchange(rows, step)
        split = other.shape[1] // 2
        halves = [
            jnp.concatenate([halves[0], other[:, :split]], axis=1),
            jnp.concatenate([halves[1], other[:, split:]], axis=1),
        ]
        rows = jnp.concatenate(halves, axis=1)
    more_rows = exchange(rows, row_steps[-1])
    payloads = [payload] + [exchange(payload, o) for o in point_offsets]
    payloads = payloads + [beside] + [exchange(p, other_core) for p in payloads[1:]]

    amount = rows.shape[1]
    half = amount // 2

    def sums(kernel, name, outs, kept, *operands, more=()):
        work = kept * size * len(payloads)
        return call(
            kernel,
            name,
            [((1, outs), F32), *more],
            *operands,
            *payloads,
            limit=16 << 20,
            scratch=[pltpu.VMEM((amount, 128), BF16), pltpu.VMEM((kept, 128), F32)],
            cost=pl.CostEstimate(
                flops=2 * feats * work, bytes_accessed=1 << 16, transcendentals=2 * work
            ),
        )

    weights = ((8 * len(payloads), size), F32)
    here, weights = sums(here_kernel, "sums_here", amount, amount, rows, more=[weights])
    (send,) = sums(send_kernel, "sums_send", amount, half, more_rows, here, weights)
    (keep,) = sums(keep_kernel, "sums_keep", half, half, more_rows, weights)
    count = jnp.pad(counts, ((0, 0), (0, slots - counts.shape[1])))
    base, spots = call(
        terms_kernel,
        "terms",
        [(line, F32), ((slots, size), BF16)],
        batch,
        count,
        preview,
        slowed,
        targets,
        keep,
    )
    keep, base, spots = lax.optimization_barrier((keep, base, spots))

    back = exchange(send, row_steps[0])
    mine, send = here[:, :half] + back[:, :half], keep + back[:, half:]
    steps = [row_steps[-1]] + row_steps[1:-1][::-1]
    for step in steps[:-1]:
        both = mine + exchange(send, step)
        half = half // 2
        mine, send = both[:, :half], both[:, half:]
    other = exchange(send, steps[-1])

    new_coef, new_velocity = call(
        finish_kernel, "finish", [(line, F32)] * 2, mine, other, base, coef, spots
    )
    return new_coef.reshape(size), new_velocity.reshape(size)


def solution(mesh):
    in_specs = (
        P(("blk", "stripe"), None),
        P(("blk", "stripe")),
        P(("blk", "stripe")),
        P(("blk", "stripe")),
        P(("blk", "stripe")),
        P("blk", "stripe"),
    )
    out_specs = (P(("blk", "stripe")), P(("blk", "stripe")))
    return jax.shard_map(
        functools.partial(per_device, dict(mesh.shape)),
        mesh=mesh,
        in_specs=in_specs,
        out_specs=out_specs,
        check_vma=False,
    )
```
